32 devices in a mesh: groups: 2 (over x), orient: 16 (over z, y, core).
Axes of the slice: x: 2, y: 2, z: 4, core: 2. Of those that a mesh axis runs over, the one named last changes fastest.
Arguments:
- images: bfloat16 [8192, 16384], P(('groups', 'orient')), parts along dimension 0, may hold values from -6 to 6
- projections: bfloat16 [32, 16384], P(('groups', 'orient')), parts along dimension 0, may hold values from -0.046875 to 0.046875
- noise_weight: float32 [32768], P('groups'), parts along dimension 0, may hold values from 0.3 to 3
- lognorm: float32 [8192], P(('groups', 'orient')), parts along dimension 0, may hold values from 4 to 6
- eligible: int32 [8192, 16], P(('groups', 'orient')), parts along dimension 0, may hold values 0 or 1
Outputs:
- orient_sums: float32 [32, 16384], P(('groups', 'orient')), parts along dimension 0
The draws below stay inside these ranges and needn't reach their ends.
There are 2 independent parts, one for each index of `groups`. The reference program is written for one: setup_inputs(seed, part) draws one part's arguments, and reference() takes and returns one part's arrays. A program takes and returns all parts, laid end to end along the dimension named above; each array names one. Nothing has to cross between parts.
All inputs are finite; a program needn't handle non-finite values. No bound on the sum of `eligible` on one device may be relied on, other than what follows from the above.
Results may differ from the reference program's by a relative error of at most 0.0044.
Values may be sent and summed in bfloat16 or wider, within the bound.
A program may use at most 64 MiB of HBM per device.

```python
import math
import jax
import jax.numpy as jnp
from jax import lax

ORI_DEV = 1
FEATS = 16384
BLOCKS = 16
ORIENT = 16
IMAGES = 4096


def plant(entries, key, least, largest):
    longest = entries.shape.index(max(entries.shape))
    spots = []
    for shift in (0, 1):
        where = [jax.random.randint(jax.random.fold_in(key, axis), (), 0, length) for axis, length in enumerate(entries.shape)]
        where[longest] = (where[longest] + shift) % entries.shape[longest]
        spots.append(tuple(where))
    return entries.at[spots[0]].set(least).at[spots[1]].set(largest)


def levels(stream_key, shape, pieces, least, top_value):
    level, own = 1.0, jax.random.fold_in(stream_key, 6)
    for axis_at, parts in pieces:
        draws = jnp.exp(jax.random.uniform(jax.random.fold_in(own, axis_at), (parts,), jnp.float32, least / len(pieces), top_value / len(pieces)))
        level = level * jnp.repeat(draws, shape[axis_at] // parts).reshape([-1 if axis == axis_at else 1 for axis in range(len(shape))])
    return level


def gaussian(key, shape, spread, bound, split=(), kind=jnp.bfloat16):
    loudness = levels(key, shape, split, -0.22, 0.18) if split else 1.0
    result = jax.random.normal(key, shape, jnp.float32) * spread * loudness
    return jnp.minimum(jnp.maximum(result, -bound), bound).astype(kind)


def setup_inputs(seed: int = 0, part: int = 0) -> dict:
    seeds = jax.random.split(jax.random.key(seed), 6)
    part_splits = jax.random.split(jax.random.fold_in(seeds[5], part), 6)
    images = gaussian(part_splits[0], (IMAGES, FEATS), 1.0, 6.0, ((0, 16),))
    projections = gaussian(part_splits[1], (ORIENT, FEATS), FEATS ** -0.5, 0.046875, ((0, 16),))
    noise_weight = jnp.clip(jnp.exp(jax.random.uniform(part_splits[2], (FEATS,), jnp.float32, math.log(0.3), math.log(3.0))), 0.3, 3.0)
    lognorm = jnp.clip(4.0 + 2.0 * jax.random.uniform(part_splits[3], (IMAGES,), jnp.float32) ** levels(part_splits[3], (IMAGES,), ((0, 16),), -0.2, 0.2), 4.0, 6.0)
    eligible = plant((jax.random.randint(part_splits[4], (IMAGES, BLOCKS), 0, 4) < 3).astype(jnp.int32), jax.random.fold_in(part_splits[4], 1), 0, 1)
    return {"images": images, "projections": projections, "noise_weight": noise_weight, "lognorm": lognorm, "eligible": eligible}


def reference(images, projections, noise_weight, lognorm, eligible):
    proj_float = projections.astype(jnp.float32)
    power = jnp.sum(proj_float * proj_float * noise_weight[None, :], axis=1)
    raw = lax.dot_general(images, projections, (((1,), (1,)), ((), ())), preferred_element_type=jnp.float32)
    scores = raw - 0.5 * power[None, :]
    mask_rows = jnp.repeat(eligible, ORI_DEV, axis=1).astype(jnp.float32)
    weights = (mask_rows * jnp.exp(scores - lognorm[:, None])).astype(jnp.bfloat16)
    return lax.dot_general(weights, images, (((0,), (0,)), ((), ())), preferred_element_type=jnp.float32)
```

```python
import functools

import jax
import jax.numpy as jnp
from jax import lax
from jax.experimental import pallas as pl
from jax.experimental.pallas import tpu as pltpu
from jax.sharding import PartitionSpec as P

MESH = pl.DeviceIdType.MESH
LANES = 128


def kernel(
    outer, inner, gq, rq, iq,
    proj_ref, noise_ref, lognorm_ref, eligible_ref, images_hbm, out_ref,
    images, gathered, staged, term, core_out, core_in, inner_out, inner_in, inner_own,
    outer_out, outer_in,
    img_sem, g_send, g_recv, c_send, c_recv, i_send, i_recv, o_send, o_recv,
):
    n = outer * inner * 2
    tiles = proj_ref.shape[0]
    feats = tiles * LANES
    me = lax.axis_index("orient")
    c = me % 2
    b = (me // 2) % inner
    a = me // (2 * inner)
    sib = 1 - c

    def at(a_, b_, c_):
        return {"orient": (a_ * inner + b_) * 2 + c_}

    def slot(a_, b_, c_):
        return (c_ * inner + b_) * outer + a_

    a_others = [(a + k) % outer for k in range(1, outer)]
    b_others = [(b + k) % inner for k in range(1, inner)]

    width = feats // iq
    loads = []
    for q in range(iq):
        part = pl.ds(q * width, width)
        loads.append(pltpu.make_async_copy(images_hbm.at[:, part], images.at[:, part], img_sem.at[q]))
        loads[-1].start()

    barrier = pltpu.get_barrier_semaphore()
    peers = [at(a_, b, c) for a_ in a_others] + [at(a, b_, c) for b_ in b_others] + [at(a, b, sib)]
    for peer in peers:
        pl.semaphore_signal(barrier, inc=1, device_id=peer, device_id_type=MESH)
    pl.semaphore_wait(barrier, len(peers))

    sends = []
    grow = tiles // gq

    def push(q, row, src, to):
        rows = pl.ds(q * grow, grow)
        copy = pltpu.make_async_remote_copy(
            src_ref=src.at[rows], dst_ref=gathered.at[row, rows],
            send_sem=g_send.at[len(sends)], recv_sem=g_recv.at[q, row],
            device_id=to, device_id_type=MESH,
        )
        copy.start()
        sends.append(copy)

    def arrived(q, row):
        rows = pl.ds(q * grow, grow)
        pltpu.make_async_remote_copy(
            src_ref=gathered.at[row, rows], dst_ref=gathered.at[row, rows],
            send_sem=g_send.at[0], recv_sem=g_recv.at[q, row],
            device_id=at(a, b, sib), device_id_type=MESH,
        ).wait_recv()

    mine = slot(a, b, c)
    for q in range(gq):
        for a_ in a_others:
            push(q, mine, proj_ref, at(a_, b, c))
        for b_ in b_others:
            push(q, mine, proj_ref, at(a, b_, c))
        push(q, mine, proj_ref, at(a, b, sib))
    gathered[mine] = proj_ref[...]

    s_at = lax.broadcasted_iota(jnp.int32, (n, n), 0)
    j_at = lax.broadcasted_iota(jnp.int32, (n, n), 1)
    s_a = s_at & (outer - 1)
    s_b = lax.shift_right_logical(s_at, outer.bit_length() - 1) & (inner - 1)
    s_c = lax.shift_right_logical(s_at, (outer * inner).bit_length() - 1)
    order = ((s_a * inner + s_b) * 2 + s_c == j_at).astype(jnp.float32).astype(jnp.bfloat16)
    mask = lax.dot_general(
        order, eligible_ref[...].astype(jnp.float32).astype(jnp.bfloat16),
        (((1,), (1,)), ((), ())), preferred_element_type=jnp.float32,
    )

    for q in range(gq):
        for a_ in a_others:
            row = slot(a_, b, c)
            arrived(q, row)
            for b_ in b_others:
                push(q, row, gathered.at[row], at(a, b_, c))
            push(q, row, gathered.at[row], at(a, b, sib))
        for b_ in b_others:
            for a_ in [a] + a_others:
                row = slot(a_, b_, c)
                arrived(q, row)
                push(q, row, gathered.at[row], at(a, b, sib))

    step = 8
    raw = jnp.zeros((n, images.shape[0]), jnp.float32)
    power = jnp.zeros((n, LANES), jnp.float32)
    for q in range(gq):
        for a_ in [a] + a_others:
            for b_ in [b] + b_others:
                arrived(q, slot(a_, b_, sib))
        for i in range(iq * q // gq, iq * (q + 1) // gq):
            loads[i].wait()

        def widen(s, carry, q=q):
            staged[pl.ds(pl.multiple_of(s * tiles + q * grow, 8), grow), :] = gathered[
                s, pl.ds(q * grow, grow), :
            ].astype(jnp.float32)
            return carry

        lax.fori_loop(0, n, widen, 0)

        def score(p, carry, q=q):
            raw, power = carry
            first = q * grow + p * step
            pieces = []
            for r in range(step):
                x = staged[pl.ds(first + r, n, stride=tiles), :]
                power = power + x * x * noise_ref[pl.ds(first + r, 1), :]
                pieces.append(x.astype(jnp.bfloat16))
            piece = jnp.concatenate(pieces, axis=1)
            cols = pl.ds(pl.multiple_of(first * LANES, step * LANES), step * LANES)
            raw = raw + lax.dot_general(
                piece, images[:, cols], (((1,), (1,)), ((), ())), preferred_element_type=jnp.float32
            )
            return raw, power

        raw, power = lax.fori_loop(0, grow // step, score, (raw, power))

    scores = raw - 0.5 * jnp.sum(power, axis=1, keepdims=True)
    weights = (mask * jnp.exp(scores - lognorm_ref[...])).astype(jnp.bfloat16)

    rrow = tiles // rq
    half = n // 2

    def copy_of(src, dst, send, recv, to):
        return pltpu.make_async_remote_copy(
            src_ref=src, dst_ref=dst, send_sem=send, recv_sem=recv, device_id=to, device_id_type=MESH
        )

    def summed(s, q):
        return term[pl.ds(q * rrow * n + s, rrow, stride=n), :]

    def compute(q):
        def piece(p, carry):
            first = q * rrow + p * step
            cols = pl.ds(pl.multiple_of(first * LANES, step * LANES), step * LANES)
            t = jnp.dot(weights, images[:, cols], preferred_element_type=jnp.float32)
            for r in range(step):
                term[pl.ds(pl.multiple_of((first + r) * n, 8), n), :] = t[:, r * LANES:(r + 1) * LANES]
            return carry

        lax.fori_loop(0, rrow // step, piece, 0)
        rows = pl.ds(q * rrow, rrow)

        def pack(h, carry):
            core_out[h, rows, :] = summed(sib * half + h, q).astype(jnp.bfloat16)
            return carry

        lax.fori_loop(0, half, pack, 0)
        copy = copy_of(core_out.at[:, rows], core_in.at[:, rows], c_send.at[q], c_recv.at[q], at(a, b, sib))
        copy.start()
        return copy

    def after_core(q, copy):
        copy.wait_recv()
        rows = pl.ds(q * rrow, rrow)
        copies = []
        for k, b_ in enumerate(b_others):
            def pack(a_, carry, b_=b_):
                h = b_ * outer + a_
                value = summed(c * half + h, q) + core_in[h, rows, :].astype(jnp.float32)
                inner_out[b_, a_, rows, :] = value.astype(jnp.bfloat16)
                return carry

            lax.fori_loop(0, outer, pack, 0)
            copies.append(copy_of(
                inner_out.at[b_, :, rows], inner_in.at[k, :, rows], i_send.at[q, k], i_recv.at[q, k], at(a, b_, c)
            ))
            copies[-1].start()

        def keep(a_, carry):
            h = b * outer + a_
            inner_own[a_, rows, :] = summed(c * half + h, q) + core_in[h, rows, :].astype(jnp.float32)
            return carry

        lax.fori_loop(0, outer, keep, 0)
        return copies

    def after_inner(q, copies):
        for copy in copies:
            copy.wait_recv()
        rows = pl.ds(q * rrow, rrow)

        def total(a_):
            value = inner_own[a_, rows, :]
            for k in range(inner - 1):
                value = value + inner_in[k, a_, rows, :].astype(jnp.float32)
            return value

        done = []
        for k, a_ in enumerate(a_others):
            outer_out[k, rows, :] = total(a_).astype(jnp.bfloat16)
            done.append(copy_of(
                outer_out.at[k, rows], outer_in.at[k, rows], o_send.at[q, k], o_recv.at[q, k], at(a_, b, c)
            ))
            done[-1].start()
        out_ref[rows, :] = total(a)
        return done

    def after_outer(q, copies):
        rows = pl.ds(q * rrow, rrow)
        value = out_ref[rows, :]
        for k, copy in enumerate(copies):
            copy.wait_recv()
            value = value + outer_in[k, rows, :].astype(jnp.float32)
        out_ref[rows, :] = value

    core_copies, inner_copies, outer_copies = {}, {}, {}
    for t in range(rq + 2):
        if t < rq:
            core_copies[t] = compute(t)
        if 0 <= t - 1 < rq:
            inner_copies[t - 1] = after_core(t - 1, core_copies[t - 1])
        if 0 <= t - 2 < rq:
            outer_copies[t - 2] = after_inner(t - 2, inner_copies[t - 2])
    for q in range(rq):
        after_outer(q, outer_copies[q])

    for copy in sends:
        copy.wait_send()
    for q in range(rq):
        for copy in [core_copies[q]] + inner_copies[q] + outer_copies[q]:
            copy.wait_send()


def body(n, images, projections, noise_weight, lognorm, eligible):
    count, feats = images.shape
    tiles = feats // LANES
    chips = n // 2
    inner = 2 ** ((chips.bit_length() - 1) // 2)
    outer = chips // inner
    gq, rq, iq = 2, 4, 4
    half = n // 2
    copies = gq * (n - 1)
    vmem = pl.BlockSpec(memory_space=pltpu.VMEM)
    dma = pltpu.SemaphoreType.DMA
    out = pl.pallas_call(
        functools.partial(kernel, outer, inner, gq, rq, iq),
        out_shape=jax.ShapeDtypeStruct((tiles, LANES), jnp.float32),
        in_specs=[vmem, vmem, vmem, vmem, pl.BlockSpec(memory_space=pl.ANY)],
        out_specs=vmem,
        scratch_shapes=[
            pltpu.VMEM((count, feats), jnp.bfloat16),
            pltpu.VMEM((n, tiles, LANES), jnp.bfloat16),
            pltpu.VMEM((n * tiles, LANES), jnp.float32),
            pltpu.VMEM((n * tiles, LANES), jnp.float32),
            pltpu.VMEM((half, tiles, LANES), jnp.bfloat16),
            pltpu.VMEM((half, tiles, LANES), jnp.bfloat16),
            pltpu.VMEM((inner, outer, tiles, LANES), jnp.bfloat16),
            pltpu.VMEM((inner - 1, outer, tiles, LANES), jnp.bfloat16),
            pltpu.VMEM((outer, tiles, LANES), jnp.float32),
            pltpu.VMEM((outer - 1, tiles, LANES), jnp.bfloat16),
            pltpu.VMEM((outer - 1, tiles, LANES), jnp.bfloat16),
            dma((iq,)),
            dma((copies,)), dma((gq, n)),
            dma((rq,)), dma((rq,)),
            dma((rq, inner - 1)), dma((rq, inner - 1)),
            dma((rq, outer - 1)), dma((rq, outer - 1)),
        ],
        compiler_params=pltpu.CompilerParams(
            collective_id=0, has_side_effects=True, vmem_limit_bytes=56 * 1024 * 1024
        ),
    )(
        projections.reshape(tiles, LANES), noise_weight.reshape(tiles, LANES),
        lognorm.reshape(1, count), eligible, images,
    )
    return out.reshape(1, feats)


def solution(mesh):
    in_specs = (
        P(("groups", "orient"), None),
        P(("groups", "orient"), None),
        P("groups"),
        P(("groups", "orient")),
        P(("groups", "orient"), None),
    )
    out_specs = P(("groups", "orient"), None)
    return jax.shard_map(
        functools.partial(body, mesh.shape["orient"]),
        mesh=mesh, in_specs=in_specs, out_specs=out_specs, check_vma=False,
    )
```

```python
import functools

import jax
import jax.numpy as jnp
from jax import lax
from jax.experimental import pallas as pl
from jax.experimental.pallas import tpu as pltpu
from jax.sharding import PartitionSpec as P

MESH = pl.DeviceIdType.MESH
LANES = 128


def kernel(
    chips, gq, rq, iq, step,
    row_ref, noise_ref, lognorm_ref, eligible_ref, images_hbm, out_ref,
    images, own_row, gathered, staged, term, core_out, core_in, chip_out, chip_in,
    img_sem, g_send, g_recv, c_send, c_recv, o_send, o_recv,
):
    n = chips * 2
    tiles = noise_ref.shape[0]
    feats = tiles * LANES
    me = lax.axis_index("orient")
    c = me % 2
    a = me // 2
    sib = 1 - c

    def at(a_, c_):
        return {"orient": a_ * 2 + c_}

    def slot(a_, c_):
        return c_ * chips + a_

    others = [(a + k) % chips for k in range(1, chips)]

    width = feats // iq
    loads = []
    for q in range(iq):
        part = pl.ds(q * width, width)
        loads.append(pltpu.make_async_copy(images_hbm.at[:, part], images.at[:, part], img_sem.at[q]))
        loads[-1].start()

    barrier = pltpu.get_barrier_semaphore()
    for peer in [at(a_, c) for a_ in others] + [at(a, sib)]:
        pl.semaphore_signal(barrier, inc=1, device_id=peer, device_id_type=MESH)

    mine = slot(a, c)
    base = pl.multiple_of(mine * tiles, 8)
    wide = row_ref[...].astype(jnp.float32)
    for r in range(tiles):
        staged[pl.ds(base + r, 1), :] = wide[:, r * LANES:(r + 1) * LANES]
    own_row[...] = staged[pl.ds(base, tiles), :].astype(jnp.bfloat16)

    pl.semaphore_wait(barrier, chips)

    sends = []
    grow = tiles // gq

    def push(q, row, src, to):
        rows = pl.ds(q * grow, grow)
        copy = pltpu.make_async_remote_copy(
            src_ref=src.at[rows], dst_ref=gathered.at[row, rows],
            send_sem=g_send.at[len(sends)], recv_sem=g_recv.at[q, row],
            device_id=to, device_id_type=MESH,
        )
        copy.start()
        sends.append(copy)

    def arrived(q, row):
        rows = pl.ds(q * grow, grow)
        pltpu.make_async_remote_copy(
            src_ref=gathered.at[row, rows], dst_ref=gathered.at[row, rows],
            send_sem=g_send.at[0], recv_sem=g_recv.at[q, row],
            device_id=at(a, sib), device_id_type=MESH,
        ).wait_recv()

    def widen(q, row):
        staged[pl.ds(pl.multiple_of(row * tiles + q * grow, 8), grow), :] = gathered[
            row, pl.ds(q * grow, grow), :
        ].astype(jnp.float32)

    for q in range(gq):
        for a_ in others:
            push(q, mine, own_row, at(a_, c))
        push(q, mine, own_row, at(a, sib))

    s_at = lax.broadcasted_iota(jnp.int32, (n, n), 0)
    j_at = lax.broadcasted_iota(jnp.int32, (n, n), 1)
    second = s_at >= chips
    own = jnp.where(second, (s_at - chips) * 2 + 1, s_at * 2)
    order = (own == j_at).astype(jnp.float32).astype(jnp.bfloat16)
    mask = jnp.dot(
        order, eligible_ref[...].astype(jnp.float32).astype(jnp.bfloat16),
        preferred_element_type=jnp.float32,
    )

    for q in range(gq):
        for a_ in others:
            row = slot(a_, c)
            arrived(q, row)
            push(q, row, gathered.at[row], at(a, sib))
            widen(q, row)

    raw = jnp.zeros((n, images.shape[0]), jnp.float32)
    power = jnp.zeros((n, LANES), jnp.float32)
    gstep = min(step, grow)
    for q in range(gq):
        for a_ in [a] + others:
            row = slot(a_, sib)
            arrived(q, row)
            widen(q, row)
        for i in range(iq * q // gq, iq * (q + 1) // gq):
            loads[i].wait()

        def score(p, carry, q=q):
            raw, power = carry
            first = q * grow + p * gstep
            pieces = []
            for r in range(gstep):
                x = staged[pl.ds(first + r, n, stride=tiles), :]
                power = power + x * x * noise_ref[pl.ds(first + r, 1), :]
                pieces.append(x.astype(jnp.bfloat16))
            piece = jnp.concatenate(pieces, axis=1)
            cols = pl.ds(pl.multiple_of(first * LANES, gstep * LANES), gstep * LANES)
            raw = raw + lax.dot_general(
                piece, images[:, cols], (((1,), (1,)), ((), ())), preferred_element_type=jnp.float32
            )
            return raw, power

        raw, power = lax.fori_loop(0, grow // gstep, score, (raw, power))

    scores = raw - 0.5 * jnp.sum(power, axis=1, keepdims=True)
    weights = (mask * jnp.exp(scores - lognorm_ref[...])).astype(jnp.bfloat16)

    rrow = tiles // rq
    rstep = min(step, rrow)

    def copy_of(src, dst, send, recv, to):
        return pltpu.make_async_remote_copy(
            src_ref=src, dst_ref=dst, send_sem=send, recv_sem=recv, device_id=to, device_id_type=MESH
        )

    def summed(s, q):
        return term[pl.ds(q * rrow * n + s, rrow, stride=n), :]

    def compute(q):
        def piece(p, carry):
            first = q * rrow + p * rstep
            cols = pl.ds(pl.multiple_of(first * LANES, rstep * LANES), rstep * LANES)
            t = jnp.dot(weights, images[:, cols], preferred_element_type=jnp.float32)
            for r in range(rstep):
                term[pl.ds(pl.multiple_of((first + r) * n, 8), n), :] = t[:, r * LANES:(r + 1) * LANES]
            return carry

        lax.fori_loop(0, rrow // rstep, piece, 0)
        rows = pl.ds(q * rrow, rrow)

        def pack(h, carry):
            core_out[h, rows, :] = summed(sib * chips + h, q).astype(jnp.bfloat16)
            return carry

        lax.fori_loop(0, chips, pack, 0, unroll=8)
        copy = copy_of(core_out.at[:, rows], core_in.at[:, rows], c_send.at[q], c_recv.at[q], at(a, sib))
        copy.start()
        return copy

    def after_core(q, copy):
        copy.wait_recv()
        rows = pl.ds(q * rrow, rrow)

        def total(a_):
            return summed(c * chips + a_, q) + core_in[a_, rows, :].astype(jnp.float32)

        copies = []
        for k, a_ in enumerate(others):
            chip_out[k, rows, :] = total(a_).astype(jnp.bfloat16)
            copies.append(copy_of(
                chip_out.at[k, rows], chip_in.at[k, rows], o_send.at[q, k], o_recv.at[q, k], at(a_, c)
            ))
            copies[-1].start()
        out_ref[rows, :] = total(a)
        return copies

    def after_chips(q, copies):
        rows = pl.ds(q * rrow, rrow)
        value = out_ref[rows, :]
        for k, copy in enumerate(copies):
            copy.wait_recv()
            value = value + chip_in[k, rows, :].astype(jnp.float32)
        out_ref[rows, :] = value

    core_copies, chip_copies = {}, {}
    for t in range(rq + 1):
        if t < rq:
            core_copies[t] = compute(t)
        if t > 0:
            chip_copies[t - 1] = after_core(t - 1, core_copies[t - 1])
    for q in range(rq):
        after_chips(q, chip_copies[q])

    for copy in sends:
        copy.wait_send()
    for q in range(rq):
        for copy in [core_copies[q]] + chip_copies[q]:
            copy.wait_send()


def body(n, images, projections, noise_weight, lognorm, eligible):
    count, feats = images.shape
    tiles = feats // LANES
    chips = n // 2
    gq, rq, iq, step = 1, 2, 4, 32
    copies = gq * (n - 1)
    vmem = pl.BlockSpec(memory_space=pltpu.VMEM)
    dma = pltpu.SemaphoreType.DMA
    out = pl.pallas_call(
        functools.partial(kernel, chips, gq, rq, iq, step),
        out_shape=pltpu.VMEM((tiles, LANES), jnp.float32),
        in_specs=[vmem, vmem, vmem, vmem, pl.BlockSpec(memory_space=pl.ANY)],
        out_specs=vmem,
        scratch_shapes=[
            pltpu.VMEM((count, feats), jnp.bfloat16),
            pltpu.VMEM((tiles, LANES), jnp.bfloat16),
            pltpu.VMEM((n, tiles, LANES), jnp.bfloat16),
            pltpu.VMEM((n * tiles, LANES), jnp.float32),
            pltpu.VMEM((n * tiles, LANES), jnp.float32),
            pltpu.VMEM((chips, tiles, LANES), jnp.bfloat16),
            pltpu.VMEM((chips, tiles, LANES), jnp.bfloat16),
            pltpu.VMEM((chips - 1, tiles, LANES), jnp.bfloat16),
            pltpu.VMEM((chips - 1, tiles, LANES), jnp.bfloat16),
            dma((iq,)),
            dma((copies,)), dma((gq, n)),
            dma((rq,)), dma((rq,)),
            dma((rq, chips - 1)), dma((rq, chips - 1)),
        ],
        compiler_params=pltpu.CompilerParams(
            collective_id=0, has_side_effects=True, vmem_limit_bytes=56 * 1024 * 1024
        ),
    )(
        projections, noise_weight.reshape(tiles, LANES),
        lognorm.reshape(1, count), eligible.T, images,
    )
    return out.reshape(1, feats)


def solution(mesh):
    in_specs = (
        P(("groups", "orient"), None),
        P(("groups", "orient"), None),
        P("groups"),
        P(("groups", "orient")),
        P(("groups", "orient"), None),
    )
    out_specs = P(("groups", "orient"), None)
    return jax.shard_map(
        functools.partial(body, mesh.shape["orient"]),
        mesh=mesh, in_specs=in_specs, out_specs=out_specs, check_vma=False,
    )
```

```python
import functools

import jax
import jax.numpy as jnp
from jax import lax
from jax.experimental import pallas as pl
from jax.experimental.pallas import tpu as pltpu
from jax.sharding import PartitionSpec as P

MESH = pl.DeviceIdType.MESH
LANES = 128


def kernel(
    chips, gq, rq, iq, step,
    row_ref, noise_ref, lognorm_ref, eligible_ref, images_hbm, out_ref,
    images, own_row, gathered, staged, term, core_out, core_in, chip_out, chip_in,
    img_sem, g_send, g_recv, c_send, c_recv, o_send, o_recv,
):
    n = chips * 2
    tiles = noise_ref.shape[0]
    feats = tiles * LANES
    me = lax.axis_index("orient")
    c = me % 2
    a = me // 2
    sib = 1 - c

    def at(a_, c_):
        return {"orient": a_ * 2 + c_}

    def slot(a_, c_):
        return c_ * chips + a_

    others = [(a + k) % chips for k in range(1, chips)]

    width = feats // iq
    loads = []
    for q in range(iq):
        part = pl.ds(q * width, width)
        loads.append(pltpu.make_async_copy(images_hbm.at[:, part], images.at[:, part], img_sem.at[q]))
        loads[-1].start()

    barrier = pltpu.get_barrier_semaphore()
    for peer in [at(a_, c) for a_ in others] + [at(a, sib)]:
        pl.semaphore_signal(barrier, inc=1, device_id=peer, device_id_type=MESH)

    mine = slot(a, c)
    base = pl.multiple_of(mine * tiles, 8)
    wide = row_ref[...].astype(jnp.float32)
    for r in range(tiles):
        staged[pl.ds(base + r, 1), :] = wide[:, r * LANES:(r + 1) * LANES]
    own_row[...] = staged[pl.ds(base, tiles), :].astype(jnp.bfloat16)

    pl.semaphore_wait(barrier, chips)

    sends = []
    grow = tiles // gq

    def push(q, row, src, to):
        rows = pl.ds(q * grow, grow)
        copy = pltpu.make_async_remote_copy(
            src_ref=src.at[rows], dst_ref=gathered.at[row, rows],
            send_sem=g_send.at[len(sends)], recv_sem=g_recv.at[q, row],
            device_id=to, device_id_type=MESH,
        )
        copy.start()
        sends.append(copy)

    def arrived(q, row):
        rows = pl.ds(q * grow, grow)
        pltpu.make_async_remote_copy(
            src_ref=gathered.at[row, rows], dst_ref=gathered.at[row, rows],
            send_sem=g_send.at[0], recv_sem=g_recv.at[q, row],
            device_id=at(a, sib), device_id_type=MESH,
        ).wait_recv()

    def widen(q, row):
        staged[pl.ds(pl.multiple_of(row * tiles + q * grow, 8), grow), :] = gathered[
            row, pl.ds(q * grow, grow), :
        ].astype(jnp.float32)

    for q in range(gq):
        for a_ in others:
            push(q, mine, own_row, at(a_, c))
        push(q, mine, own_row, at(a, sib))

    s_at = lax.broadcasted_iota(jnp.int32, (n, n), 0)
    j_at = lax.broadcasted_iota(jnp.int32, (n, n), 1)
    second = s_at >= chips
    own = jnp.where(second, (s_at - chips) * 2 + 1, s_at * 2)
    order = (own == j_at).astype(jnp.float32).astype(jnp.bfloat16)
    mask = jnp.dot(
        order, eligible_ref[...].astype(jnp.float32).astype(jnp.bfloat16),
        preferred_element_type=jnp.float32,
    )

    for q in range(gq):
        for a_ in others:
            row = slot(a_, c)
            arrived(q, row)
            push(q, row, gathered.at[row], at(a, sib))
            widen(q, row)

    raw = jnp.zeros((n, images.shape[0]), jnp.float32)
    power = jnp.zeros((n, LANES), jnp.float32)
    gstep = min(step, grow)
    for q in range(gq):
        for a_ in [a] + others:
            row = slot(a_, sib)
            arrived(q, row)
            widen(q, row)
        for i in range(iq * q // gq, iq * (q + 1) // gq):
            loads[i].wait()

        def score(p, carry, q=q):
            raw, power = carry
            first = q * grow + p * gstep
            pieces = []
            for r in range(gstep):
                x = staged[pl.ds(first + r, n, stride=tiles), :]
                power = power + x * x * noise_ref[pl.ds(first + r, 1), :]
                pieces.append(x.astype(jnp.bfloat16))
            piece = jnp.concatenate(pieces, axis=1)
            cols = pl.ds(pl.multiple_of(first * LANES, gstep * LANES), gstep * LANES)
            raw = raw + lax.dot_general(
                piece, images[:, cols], (((1,), (1,)), ((), ())), preferred_element_type=jnp.float32
            )
            return raw, power

        raw, power = lax.fori_loop(0, grow // gstep, score, (raw, power))

    scores = raw - 0.5 * jnp.sum(power, axis=1, keepdims=True)
    weights = (mask * jnp.exp(scores - lognorm_ref[...])).astype(jnp.bfloat16)

    rrow = tiles // rq
    rstep = min(step, rrow)

    def copy_of(src, dst, send, recv, to):
        return pltpu.make_async_remote_copy(
            src_ref=src, dst_ref=dst, send_sem=send, recv_sem=recv, device_id=to, device_id_type=MESH
        )

    def summed(s, q):
        return term[pl.ds(q * rrow * n + s, rrow, stride=n), :]

    def compute(q):
        def piece(p, carry):
            first = q * rrow + p * rstep
            cols = pl.ds(pl.multiple_of(first * LANES, rstep * LANES), rstep * LANES)
            t = jnp.dot(weights, images[:, cols], preferred_element_type=jnp.float32)
            for r in range(rstep):
                term[pl.ds(pl.multiple_of((first + r) * n, 8), n), :] = t[:, r * LANES:(r + 1) * LANES]
            return carry

        lax.fori_loop(0, rrow // rstep, piece, 0)
        rows = pl.ds(q * rrow, rrow)

        def pack(h, carry):
            core_out[h, rows, :] = summed(sib * chips + h, q).astype(jnp.bfloat16)
            return carry

        lax.fori_loop(0, chips, pack, 0, unroll=8)
        copy = copy_of(core_out.at[:, rows], core_in.at[:, rows], c_send.at[q], c_recv.at[q], at(a, sib))
        copy.start()
        return copy

    def after_core(q, copy):
        copy.wait_recv()
        rows = pl.ds(q * rrow, rrow)

        def total(a_):
            return summed(c * chips + a_, q) + core_in[a_, rows, :].astype(jnp.float32)

        copies = []
        for k, a_ in enumerate(others):
            chip_out[k, rows, :] = total(a_).astype(jnp.bfloat16)
            copies.append(copy_of(
                chip_out.at[k, rows], chip_in.at[k, rows], o_send.at[q, k], o_recv.at[q, k], at(a_, c)
            ))
            copies[-1].start()
        out_ref[rows, :] = total(a)
        return copies

    def after_chips(q, copies):
        rows = pl.ds(q * rrow, rrow)
        value = out_ref[rows, :]
        for k, copy in enumerate(copies):
            copy.wait_recv()
            value = value + chip_in[k, rows, :].astype(jnp.float32)
        out_ref[rows, :] = value

    core_copies, chip_copies = {}, {}
    for t in range(rq + 1):
        if t < rq:
            core_copies[t] = compute(t)
        if t > 0:
            chip_copies[t - 1] = after_core(t - 1, core_copies[t - 1])
    for q in range(rq):
        after_chips(q, chip_copies[q])

    for copy in sends:
        copy.wait_send()
    for q in range(rq):
        for copy in [core_copies[q]] + chip_copies[q]:
            copy.wait_send()


def body(n, images, projections, noise_weight, lognorm, eligible):
    count, feats = images.shape
    tiles = feats // LANES
    chips = n // 2
    gq, rq, iq, step = 2, 4, 4, 32
    copies = gq * (n - 1)
    vmem = pl.BlockSpec(memory_space=pltpu.VMEM)
    dma = pltpu.SemaphoreType.DMA
    out = pl.pallas_call(
        functools.partial(kernel, chips, gq, rq, iq, step),
        out_shape=pltpu.VMEM((tiles, LANES), jnp.float32),
        in_specs=[vmem, vmem, vmem, vmem, pl.BlockSpec(memory_space=pl.ANY)],
        out_specs=vmem,
        scratch_shapes=[
            pltpu.VMEM((count, feats), jnp.bfloat16),
            pltpu.VMEM((tiles, LANES), jnp.bfloat16),
            pltpu.VMEM((n, tiles, LANES), jnp.bfloat16),
            pltpu.VMEM((n * tiles, LANES), jnp.float32),
            pltpu.VMEM((n * tiles, LANES), jnp.float32),
            pltpu.VMEM((chips, tiles, LANES), jnp.bfloat16),
            pltpu.VMEM((chips, tiles, LANES), jnp.bfloat16),
            pltpu.VMEM((chips - 1, tiles, LANES), jnp.bfloat16),
            pltpu.VMEM((chips - 1, tiles, LANES), jnp.bfloat16),
            dma((iq,)),
            dma((copies,)), dma((gq, n)),
            dma((rq,)), dma((rq,)),
            dma((rq, chips - 1)), dma((rq, chips - 1)),
        ],
        compiler_params=pltpu.CompilerParams(
            collective_id=0, has_side_effects=True, vmem_limit_bytes=56 * 1024 * 1024
        ),
    )(
        projections, noise_weight.reshape(tiles, LANES),
        lognorm.reshape(1, count), eligible.T, images,
    )
    return out.reshape(1, feats)


def solution(mesh):
    in_specs = (
        P(("groups", "orient"), None),
        P(("groups", "orient"), None),
        P("groups"),
        P(("groups", "orient")),
        P(("groups", "orient"), None),
    )
    out_specs = P(("groups", "orient"), None)
    return jax.shard_map(
        functools.partial(body, mesh.shape["orient"]),
        mesh=mesh, in_specs=in_specs, out_specs=out_specs, check_vma=False,
    )
```
